32 devices in a mesh: sector: 4 (over x, core), tile: 8 (over z, y).
Axes of the slice: x: 2, y: 2, z: 4, core: 2. Of those that a mesh axis runs over, the one named last changes fastest.
Arguments:
- snapshots: bfloat16 [4, 30720, 384], P(None, ('sector', 'tile')), may hold values from -6 to 6
- density: float32 [30720], P(('sector', 'tile')), may hold values from 0.5 to 2
- sound_speed: float32 [30720], P(('sector', 'tile')), may hold values from 0.5 to 2
- offsets: int32 [30720], P(('sector', 'tile')), may hold values from -32 to 32
- rotation: bfloat16 [384, 128], P('tile'), may hold values from -0.3125 to 0.3125
Outputs:
- projection: float32 [4, 384, 128], replicated
The draws below stay inside these ranges and needn't reach their ends.
All inputs are finite; a program needn't handle non-finite values.
Results may differ from the reference program's by a relative error of at most 0.0003.
Values may be sent and summed in bfloat16 or wider, within the bound.
A program may use at most 64 MiB of HBM per device.

```python
import math
import jax
import jax.numpy as jnp
from jax import lax

K = 384
M = 128
CL = 960
HALO = 32
NC = 30720


def set_ends(values, own_key, smallest, top_value):
    index_at = [jax.random.randint(jax.random.fold_in(own_key, axis), (), 0, length) for axis, length in enumerate(values.shape)]
    longest = values.shape.index(max(values.shape))
    beside = index_at[:longest] + [(index_at[longest] + 1) % values.shape[longest]] + index_at[longest + 1:]
    return values.at[tuple(index_at)].set(smallest).at[tuple(beside)].set(top_value)


def level_of(rng, shape, cuts, smallest, top_value):
    def one(axis_at, shards_of):
        steps = jax.random.uniform(jax.random.fold_in(jax.random.fold_in(rng, 6), axis_at), (shards_of,), jnp.float32, smallest / len(cuts), top_value / len(cuts))
        return jnp.repeat(jnp.exp(steps), shape[axis_at] // shards_of).reshape((-1,) + (1,) * (len(shape) - axis_at - 1))

    factor_of = one(*cuts[0])
    for cut in cuts[1:]:
        factor_of = factor_of * one(*cut)
    return factor_of


def bell_draw(rng, extent, deviation, limit, split=(), held_as=jnp.bfloat16):
    level = level_of(rng, extent, split, -0.22, 0.18) if split else 1.0
    array = jax.random.normal(rng, extent, jnp.float32) * deviation * level
    return jnp.minimum(jnp.maximum(array, -limit), limit).astype(held_as)


def setup_inputs(seed: int = 0) -> dict:
    key_list = jax.random.split(jax.random.key(seed), 6)
    return {
        "snapshots": bell_draw(key_list[0], (4, NC, K), 1.0, 6.0, ((1, 32),)),
        "density": jnp.clip(jnp.exp(math.log(2.0) - 1.3862944 * jax.random.uniform(key_list[1], (NC,), jnp.float32) ** level_of(key_list[1], (NC,), ((0, 32),), -0.2, 0.2)), 0.5, 2.0),
        "sound_speed": jnp.clip(jnp.exp(math.log(2.0) - 1.3862944 * jax.random.uniform(key_list[2], (NC,), jnp.float32) ** level_of(key_list[2], (NC,), ((0, 32),), -0.2, 0.2)), 0.5, 2.0),
        "offsets": set_ends(jax.random.randint(key_list[3], (NC,), -HALO, HALO + 1), jax.random.fold_in(key_list[3], 1), -HALO, HALO).astype(jnp.int32),
        "rotation": bell_draw(key_list[4], (K, M), K ** -0.5, 0.3125, ((0, 8),)),
    }


def weighting(local_cells, near_press, near_sum, density, sound_speed):
    local_wide = local_cells.astype(jnp.float32)
    inverse = 1.0 / (density * sound_speed * sound_speed)
    vel_local = local_wide[1] + local_wide[2] + local_wide[3]
    potential = local_wide[0] * inverse + 0.5 * (near_sum - vel_local) / sound_speed
    kinetic = density[None] * local_wide[1:] + 0.5 * (near_press - local_wide[0])[None] / sound_speed[None]
    return jnp.concatenate([potential[None], kinetic], axis=0).astype(jnp.bfloat16)

def reference(snapshots, density, sound_speed, offsets, rotation):

    def block_terms(carry, first_cell):
        cell_rows = first_cell + jnp.arange(CL, dtype=jnp.int32)
        shift_rows = lax.dynamic_slice_in_dim(offsets, first_cell, CL)
        neighbor_rows = jnp.mod(cell_rows + shift_rows, NC).astype(jnp.int32)
        local_cells = lax.dynamic_slice_in_dim(snapshots, first_cell, CL, 1)
        neighbors = jnp.take(snapshots, neighbor_rows, axis=1).astype(jnp.float32)
        near_press = neighbors[0]
        near_sum = neighbors[1] + neighbors[2] + neighbors[3]
        dens_rows = lax.dynamic_slice_in_dim(density, first_cell, CL)[:, None]
        speed_rows = lax.dynamic_slice_in_dim(sound_speed, first_cell, CL)[:, None]
        weighted = weighting(local_cells, near_press, near_sum, dens_rows, speed_rows)
        mode_fields = jnp.dot(local_cells.reshape(4 * CL, K), rotation, preferred_element_type=jnp.float32)
        mode_fields = mode_fields.astype(jnp.bfloat16).reshape(4, CL, M)
        parts = [jnp.dot(weighted[component].T, mode_fields[component], preferred_element_type=jnp.float32) for component in range(4)]
        return (carry + jnp.stack(parts, axis=0), None)
    starts = jnp.arange(NC // CL, dtype=jnp.int32) * CL
    initial = jnp.zeros((4, K, M), jnp.float32)
    summed, _ = lax.scan(block_terms, initial, starts)
    return summed / math.sqrt(NC)
```

```python
import functools
import math

import jax
import jax.numpy as jnp
from jax import lax
from jax.experimental import pallas as pl
from jax.experimental.pallas import tpu as pltpu
from jax.sharding import PartitionSpec as P

HALO = 32
GROUP = 8
BLOCK = 192
CHUNK = 128
MESH = pl.DeviceIdType.MESH


def remote(src, dst, send_sem, recv_sem, device):
    return pltpu.make_async_remote_copy(
        src_ref=src,
        dst_ref=dst,
        send_sem=send_sem,
        recv_sem=recv_sem,
        device_id=device,
        device_id_type=MESH,
    )


def kernel(
    sectors, tiles, gather_rotation,
    snap_ref, dens_ref, speed_ref, off_ref, rot_ref,
    out_ref,
    pad, rows, weighted, fields, rot_all, part, core_in, x_out, x_in, own, slots, far,
    load_sem, halo_send, halo_recv, rot_send, rot_recv, core_send, core_recv, x_send, x_recv,
    rs_send, rs_recv, far_send, far_recv, ag_send, ag_recv, agx_send, agx_recv, agc_send, agc_recv,
):
    comps, cells, snaps = snap_ref.shape
    chunks = snaps // CHUNK
    share = CHUNK // GROUP
    groups = tiles // GROUP
    cell_total = cells * sectors * tiles

    s = lax.axis_index("sector")
    t = lax.axis_index("tile")
    core = lax.rem(s, 2)
    side = s // 2
    low = lax.rem(t, GROUP)
    high = t // GROUP
    comp = 2 * core + side
    other_core = (s + 1 - 2 * core, t)
    other_side = (lax.rem(s + 2, sectors), t)

    def group_tile(step):
        return high * GROUP + lax.rem(low + step, GROUP)

    def far_tile(step):
        return lax.rem(high + step, groups) * GROUP + low

    me = s * tiles + t
    total = sectors * tiles
    right_index = lax.rem(me + 1, total)
    left_index = lax.rem(me + total - 1, total)
    right = (right_index // tiles, lax.rem(right_index, tiles))
    left = (left_index // tiles, lax.rem(left_index, tiles))

    loads = [
        pltpu.make_async_copy(
            snap_ref.at[c], pad.at[c, pl.ds(HALO, cells)], load_sem.at[c]
        )
        for c in range(comps)
    ]
    for load in loads:
        load.start()

    peers = [left, right, other_core, other_side]
    peers += [(s, group_tile(d)) for d in range(1, GROUP)]
    peers += [(s, far_tile(e)) for e in range(1, groups)]
    barrier = pltpu.get_barrier_semaphore()
    for peer in peers:
        pl.semaphore_signal(barrier, inc=1, device_id=peer, device_id_type=MESH)

    rows[...] = jnp.zeros_like(rows)
    dens = dens_ref[...]
    speed = speed_ref[...]
    rows[0:1, 0:cells] = dens
    rows[1:2, 0:cells] = 1.0 / (dens * speed * speed)
    rows[2:3, 0:cells] = 0.5 / speed
    rows[3:4, 0:cells] = off_ref[...].astype(jnp.float32) + HALO
    columns = rows[...].T

    pl.semaphore_wait(barrier, len(peers))
    sends = []
    depth = rot_ref.shape[0]
    if gather_rotation:
        def rot_at(tile):
            return pl.ds(pl.multiple_of(tile * depth, 16), depth)

        for d in range(1, tiles):
            copy = remote(
                rot_ref, rot_all.at[rot_at(t)], rot_send.at[d], rot_recv.at[d],
                (s, lax.rem(t + d, tiles)),
            )
            copy.start()
            sends.append(copy)
        rot_all[rot_at(t), :] = rot_ref[...]
    else:
        rot_all[...] = rot_ref[...]
    to_right = remote(
        snap_ref.at[:, pl.ds(cells - HALO, HALO)], pad.at[:, pl.ds(0, HALO)],
        halo_send.at[0], halo_recv.at[0], right,
    )
    to_left = remote(
        snap_ref.at[:, pl.ds(0, HALO)], pad.at[:, pl.ds(HALO + cells, HALO)],
        halo_send.at[1], halo_recv.at[1], left,
    )
    to_right.start()
    to_left.start()
    sends += [to_right, to_left]

    window = BLOCK + 2 * HALO
    shift = (
        lax.broadcasted_iota(jnp.int32, (BLOCK, window), 1)
        - lax.broadcasted_iota(jnp.int32, (BLOCK, window), 0)
    ).astype(jnp.float32)
    own_cell = jnp.where(shift == HALO, 1.0, 0.0)

    def weigh(block):
        first = block * BLOCK
        column = columns[first : first + BLOCK]
        dens_c, inverse, slope, target = (column[:, i : i + 1] for i in range(4))
        pick = (jnp.where(shift == target, 1.0, 0.0) - own_cell).astype(jnp.bfloat16)

        def change(c):
            return jnp.dot(
                pick, pad[c, first : first + window, :], preferred_element_type=jnp.float32
            )

        def local(c):
            return pad[c, HALO + first : HALO + first + BLOCK, :].astype(jnp.float32)

        d_sum = (change(1) + change(2)) + change(3)
        weighted[0, first : first + BLOCK, :] = (
            local(0) * inverse + d_sum * slope
        ).astype(jnp.bfloat16)
        push = change(0) * slope
        for c in range(1, comps):
            weighted[c, first : first + BLOCK, :] = (dens_c * local(c) + push).astype(
                jnp.bfloat16
            )

    for load in loads:
        load.wait()
    blocks = cells // BLOCK
    for block in range(1, blocks - 1):
        weigh(block)

    if gather_rotation:
        for d in range(1, tiles):
            source = lax.rem(t + tiles - d, tiles)
            remote(
                rot_ref, rot_all.at[rot_at(source)], rot_send.at[d], rot_recv.at[d],
                (s, source),
            ).wait_recv()
    for c in range(comps):
        fields[c] = jnp.dot(
            pad[c, HALO : HALO + cells, :], rot_all[...], preferred_element_type=jnp.float32
        ).astype(jnp.bfloat16)

    to_right.wait_recv()
    to_left.wait_recv()
    weigh(0)
    weigh(blocks - 1)

    def span(q):
        return pl.ds(q * CHUNK, CHUNK)

    def shard(q, lo):
        return pl.ds(pl.multiple_of(q * CHUNK + lo * share, share), share)

    def core_copy(q):
        return remote(
            part.at[pl.ds(2 * (1 - core), 2), span(q)], core_in.at[q],
            core_send.at[q], core_recv.at[q], other_core,
        )

    def x_copy(q):
        return remote(x_out.at[q], x_in.at[q], x_send.at[q], x_recv.at[q], other_side)

    def rs_copy(q, d):
        lo = lax.rem(low + d, GROUP)
        return remote(
            own.at[q, pl.ds(pl.multiple_of(lo * share, share), share)], slots.at[q, d],
            rs_send.at[q, d], rs_recv.at[q, d], (s, group_tile(d)),
        )

    def far_copy(q, e):
        return remote(
            far.at[q, high], far.at[q, high],
            far_send.at[q, e], far_recv.at[q, e], (s, far_tile(e)),
        )

    def ag_copy(q, d):
        place = out_ref.at[comp, shard(q, low)]
        return remote(place, place, ag_send.at[q, d], ag_recv.at[q, d], (s, group_tile(d)))

    def agx_copy(q):
        place = out_ref.at[comp, span(q)]
        return remote(place, place, agx_send.at[q], agx_recv.at[q], other_side)

    def agc_copy(q):
        place = out_ref.at[pl.ds(2 * core, 2), span(q)]
        return remote(place, place, agc_send.at[q], agc_recv.at[q], other_core)

    def begin(copy):
        copy.start()
        sends.append(copy)

    def project(q):
        for c in range(comps):
            part[c, q * CHUNK : (q + 1) * CHUNK, :] = lax.dot_general(
                weighted[c, :, q * CHUNK : (q + 1) * CHUNK],
                fields[c],
                (((0,), (0,)), ((), ())),
                preferred_element_type=jnp.float32,
            )
        begin(core_copy(q))

    def over_core(q):
        core_copy(q).wait_recv()
        x_out[q] = part[2 * core + 1 - side, q * CHUNK : (q + 1) * CHUNK, :] + core_in[q, 1 - side]
        begin(x_copy(q))
        own[q] = part[comp, q * CHUNK : (q + 1) * CHUNK, :] + core_in[q, side]

    def over_side(q):
        x_copy(q).wait_recv()
        own[q] = own[q] + x_in[q]
        for d in range(1, GROUP):
            begin(rs_copy(q, d))

    def over_tiles(q):
        for d in range(1, GROUP):
            rs_copy(q, d).wait_recv()
        value = own[q, pl.ds(pl.multiple_of(low * share, share), share), :]
        for d in range(1, GROUP):
            value = value + slots[q, d]
        if groups > 1:
            far[q, high] = value
            for e in range(1, groups):
                begin(far_copy(q, e))
            for e in range(1, groups):
                source = lax.rem(high + groups - e, groups)
                remote(
                    far.at[q, source], far.at[q, source],
                    far_send.at[q, e], far_recv.at[q, e], (s, far_tile(e)),
                ).wait_recv()
            value = far[q, 0]
            for e in range(1, groups):
                value = value + far[q, e]
        out_ref[comp, shard(q, low), :] = value / math.sqrt(cell_total)
        for d in range(1, GROUP):
            begin(ag_copy(q, d))

    def back_side(q):
        for d in range(1, GROUP):
            place = out_ref.at[comp, shard(q, lax.rem(low + GROUP - d, GROUP))]
            remote(
                place, place, ag_send.at[q, d], ag_recv.at[q, d], (s, group_tile(d))
            ).wait_recv()
        begin(agx_copy(q))

    def back_core(q):
        place = out_ref.at[2 * core + 1 - side, span(q)]
        remote(place, place, agx_send.at[q], agx_recv.at[q], other_side).wait_recv()
        begin(agc_copy(q))

    def finish(q):
        place = out_ref.at[pl.ds(2 * (1 - core), 2), span(q)]
        remote(place, place, agc_send.at[q], agc_recv.at[q], other_core).wait_recv()

    stages = [project, over_core, over_side, over_tiles, back_side, back_core, finish]
    for step in range(chunks + len(stages) - 1):
        for index, stage in enumerate(stages):
            if 0 <= step - index < chunks:
                stage(step - index)
    for copy in sends:
        copy.wait_send()


def on_device(sectors, tiles, snapshots, density, sound_speed, offsets, rotation):
    comps, cells, snaps = snapshots.shape
    gather_rotation = rotation.shape[0] % 16 == 0
    if not gather_rotation:
        rotation = lax.all_gather(rotation, "tile", axis=0, tiled=True)
    modes = rotation.shape[1]
    chunks = snaps // CHUNK
    share = CHUNK // GROUP
    groups = tiles // GROUP
    wide = -(-cells // 128) * 128
    f32, bf16 = jnp.float32, jnp.bfloat16
    dma = pltpu.SemaphoreType.DMA
    vmem = pl.BlockSpec(memory_space=pltpu.VMEM)
    return pl.pallas_call(
        functools.partial(kernel, sectors, tiles, gather_rotation),
        out_shape=jax.ShapeDtypeStruct((comps, snaps, modes), f32),
        in_specs=[pl.BlockSpec(memory_space=pl.ANY), vmem, vmem, vmem, vmem],
        out_specs=vmem,
        scratch_shapes=[
            pltpu.VMEM((comps, cells + 2 * HALO, snaps), bf16),
            pltpu.VMEM((8, wide), f32),
            pltpu.VMEM((comps, cells, snaps), bf16),
            pltpu.VMEM((comps, cells, modes), bf16),
            pltpu.VMEM((snaps, modes), bf16),
            pltpu.VMEM((comps, snaps, modes), f32),
            pltpu.VMEM((chunks, 2, CHUNK, modes), f32),
            pltpu.VMEM((chunks, CHUNK, modes), f32),
            pltpu.VMEM((chunks, CHUNK, modes), f32),
            pltpu.VMEM((chunks, CHUNK, modes), f32),
            pltpu.VMEM((chunks, GROUP, share, modes), f32),
            pltpu.VMEM((chunks, groups, share, modes), f32),
            dma((comps,)),
            dma((2,)),
            dma((2,)),
            dma((tiles,)),
            dma((tiles,)),
            dma((chunks,)),
            dma((chunks,)),
            dma((chunks,)),
            dma((chunks,)),
            dma((chunks, GROUP)),
            dma((chunks, GROUP)),
            dma((chunks, groups)),
            dma((chunks, groups)),
            dma((chunks, GROUP)),
            dma((chunks, GROUP)),
            dma((chunks,)),
            dma((chunks,)),
            dma((chunks,)),
            dma((chunks,)),
        ],
        compiler_params=pltpu.CompilerParams(
            collective_id=0, has_side_effects=True, vmem_limit_bytes=40 * 1024 * 1024
        ),
        cost_estimate=pl.CostEstimate(
            flops=4 * cells * comps * snaps * modes, bytes_accessed=2 * comps * cells * snaps,
            transcendentals=0,
        ),
    )(snapshots, density[None], sound_speed[None], offsets[None], rotation)


def solution(mesh):
    sectors, tiles = mesh.shape["sector"], mesh.shape["tile"]
    return jax.shard_map(
        functools.partial(on_device, sectors, tiles),
        mesh=mesh,
        in_specs=(
            P(None, ("sector", "tile"), None),
            P(("sector", "tile")),
            P(("sector", "tile")),
            P(("sector", "tile")),
            P("tile", None),
        ),
        out_specs=P(),
        check_vma=False,
    )
```

```python
import functools
import math

import jax
import jax.numpy as jnp
from jax import lax
from jax.experimental import pallas as pl
from jax.experimental.pallas import tpu as pltpu
from jax.sharding import PartitionSpec as P

HALO = 32
GROUP = 8
BLOCK = 192
CHUNK = 128
SPACING = 1.5
MESH = pl.DeviceIdType.MESH


def remote(src, dst, send_sem, recv_sem, device):
    return pltpu.make_async_remote_copy(
        src_ref=src,
        dst_ref=dst,
        send_sem=send_sem,
        recv_sem=recv_sem,
        device_id=device,
        device_id_type=MESH,
    )


def kernel(
    sectors, tiles, gather_rotation,
    snap_ref, dens_ref, speed_ref, off_ref, rot_ref,
    out_ref,
    dens_in, speed_in, off_in, pad, rows, weighted, fields, rot_all, part, core_in, x_out, x_in, own, slots, far,
    load_sem, cell_sem, own_rot_sem, halo_send, halo_recv, rot_send, rot_recv, core_send, core_recv, x_send, x_recv,
    rs_send, rs_recv, far_send, far_recv, ag_send, ag_recv, agx_send, agx_recv, agc_send, agc_recv,
):
    comps, cells, snaps = snap_ref.shape
    chunks = snaps // CHUNK
    share = CHUNK // GROUP
    groups = tiles // GROUP
    cell_total = cells * sectors * tiles

    s = lax.axis_index("sector")
    t = lax.axis_index("tile")
    core = lax.rem(s, 2)
    side = s // 2
    low = lax.rem(t, GROUP)
    high = t // GROUP
    comp = 2 * core + side
    other_core = (s + 1 - 2 * core, t)
    other_side = (lax.rem(s + 2, sectors), t)

    def group_tile(step):
        return high * GROUP + lax.rem(low + step, GROUP)

    def far_tile(step):
        return lax.rem(high + step, groups) * GROUP + low

    me = s * tiles + t
    total = sectors * tiles
    right_index = lax.rem(me + 1, total)
    left_index = lax.rem(me + total - 1, total)
    right = (right_index // tiles, lax.rem(right_index, tiles))
    left = (left_index // tiles, lax.rem(left_index, tiles))

    loads = [
        pltpu.make_async_copy(
            snap_ref.at[c], pad.at[c, pl.ds(HALO, cells)], load_sem.at[c]
        )
        for c in range(comps)
    ]
    cell_loads = [
        pltpu.make_async_copy(source, target, cell_sem.at[i])
        for i, (source, target) in enumerate(
            ((dens_ref, dens_in), (speed_ref, speed_in), (off_ref, off_in))
        )
    ]
    for load in cell_loads + loads:
        load.start()

    peers = [left, right, other_core, other_side]
    peers += [(s, group_tile(d)) for d in range(1, GROUP)]
    peers += [(s, far_tile(e)) for e in range(1, groups)]
    barrier = pltpu.get_barrier_semaphore()
    for peer in peers:
        pl.semaphore_signal(barrier, inc=1, device_id=peer, device_id_type=MESH)

    rows[...] = jnp.zeros_like(rows)
    for load in cell_loads:
        load.wait()
    dens = dens_in[...]
    speed = speed_in[...]
    rows[0:1, 0:cells] = dens
    rows[1:2, 0:cells] = 1.0 / (dens * speed * speed)
    rows[2:3, 0:cells] = 0.5 / speed
    rows[3:4, 0:cells] = off_in[...].astype(jnp.float32) + HALO
    columns = rows[...].T

    pl.semaphore_wait(barrier, len(peers))
    sends = []
    depth = rot_ref.shape[0]
    if gather_rotation:
        def rot_at(tile):
            return pl.ds(pl.multiple_of(tile * depth, 16), depth)

        for d in range(1, tiles):
            copy = remote(
                rot_ref, rot_all.at[rot_at(t)], rot_send.at[d], rot_recv.at[d],
                (s, lax.rem(t + d, tiles)),
            )
            copy.start()
            sends.append(copy)
        own_rot = pltpu.make_async_copy(rot_ref, rot_all.at[rot_at(t)], own_rot_sem.at[0])
    else:
        own_rot = pltpu.make_async_copy(rot_ref, rot_all, own_rot_sem.at[0])
    own_rot.start()
    to_right = remote(
        snap_ref.at[:, pl.ds(cells - HALO, HALO)], pad.at[:, pl.ds(0, HALO)],
        halo_send.at[0], halo_recv.at[0], right,
    )
    to_left = remote(
        snap_ref.at[:, pl.ds(0, HALO)], pad.at[:, pl.ds(HALO + cells, HALO)],
        halo_send.at[1], halo_recv.at[1], left,
    )
    to_right.start()
    to_left.start()
    sends += [to_right, to_left]

    window = BLOCK + 2 * HALO
    shift = (
        lax.broadcasted_iota(jnp.int32, (BLOCK, window), 1)
        - lax.broadcasted_iota(jnp.int32, (BLOCK, window), 0)
    ).astype(jnp.float32)
    own_cell = jnp.where(shift == HALO, 1.0, 0.0)

    def weigh(block, q):
        first = block * BLOCK
        lanes = slice(q * CHUNK, (q + 1) * CHUNK)
        column = columns[first : first + BLOCK]
        dens_c, inverse, slope, target = (column[:, i : i + 1] for i in range(4))
        pick = (jnp.where(shift == target, 1.0, 0.0) - own_cell).astype(jnp.bfloat16)

        def change(c):
            return jnp.dot(
                pick, pad[c, first : first + window, lanes], preferred_element_type=jnp.float32
            )

        def local(c):
            return pad[c, HALO + first : HALO + first + BLOCK, lanes].astype(jnp.float32)

        d_sum = (change(1) + change(2)) + change(3)
        weighted[0, first : first + BLOCK, lanes] = (
            local(0) * inverse + d_sum * slope
        ).astype(jnp.bfloat16)
        push = change(0) * slope
        for c in range(1, comps):
            weighted[c, first : first + BLOCK, lanes] = (dens_c * local(c) + push).astype(
                jnp.bfloat16
            )

    for load in loads:
        load.wait()
    blocks = cells // BLOCK
    for block in range(1, blocks - 1):
        weigh(block, 0)

    if gather_rotation:
        for d in range(1, tiles):
            source = lax.rem(t + tiles - d, tiles)
            remote(
                rot_ref, rot_all.at[rot_at(source)], rot_send.at[d], rot_recv.at[d],
                (s, source),
            ).wait_recv()
    own_rot.wait()
    for c in range(comps):
        fields[c] = jnp.dot(
            pad[c, HALO : HALO + cells, :], rot_all[...], preferred_element_type=jnp.float32
        ).astype(jnp.bfloat16)

    to_right.wait_recv()
    to_left.wait_recv()
    weigh(0, 0)
    weigh(blocks - 1, 0)

    def span(q):
        return pl.ds(q * CHUNK, CHUNK)

    def shard(q, lo):
        return pl.ds(pl.multiple_of(q * CHUNK + lo * share, share), share)

    def core_copy(q):
        return remote(
            part.at[pl.ds(2 * (1 - core), 2), span(q)], core_in.at[q],
            core_send.at[q], core_recv.at[q], other_core,
        )

    def x_copy(q):
        return remote(x_out.at[q], x_in.at[q], x_send.at[q], x_recv.at[q], other_side)

    def rs_copy(q, d):
        lo = lax.rem(low + d, GROUP)
        return remote(
            own.at[q, pl.ds(pl.multiple_of(lo * share, share), share)], slots.at[q, d],
            rs_send.at[q, d], rs_recv.at[q, d], (s, group_tile(d)),
        )

    def far_copy(q, e):
        return remote(
            far.at[q, high], far.at[q, high],
            far_send.at[q, e], far_recv.at[q, e], (s, far_tile(e)),
        )

    def ag_copy(q, d):
        place = out_ref.at[comp, shard(q, low)]
        return remote(place, place, ag_send.at[q, d], ag_recv.at[q, d], (s, group_tile(d)))

    def agx_copy(q):
        place = out_ref.at[comp, span(q)]
        return remote(place, place, agx_send.at[q], agx_recv.at[q], other_side)

    def agc_copy(q):
        place = out_ref.at[pl.ds(2 * core, 2), span(q)]
        return remote(place, place, agc_send.at[q], agc_recv.at[q], other_core)

    def begin(copy):
        copy.start()
        sends.append(copy)

    def project(q):
        if q > 0:
            for block in range(blocks):
                weigh(block, q)
        for c in range(comps):
            part[c, q * CHUNK : (q + 1) * CHUNK, :] = lax.dot_general(
                weighted[c, :, q * CHUNK : (q + 1) * CHUNK],
                fields[c],
                (((0,), (0,)), ((), ())),
                preferred_element_type=jnp.float32,
            )
        begin(core_copy(q))

    def over_core(q):
        core_copy(q).wait_recv()
        x_out[q] = part[2 * core + 1 - side, q * CHUNK : (q + 1) * CHUNK, :] + core_in[q, 1 - side]
        begin(x_copy(q))
        own[q] = part[comp, q * CHUNK : (q + 1) * CHUNK, :] + core_in[q, side]

    def over_side(q):
        x_copy(q).wait_recv()
        own[q] = own[q] + x_in[q]
        for d in range(1, GROUP):
            begin(rs_copy(q, d))

    def over_tiles(q):
        for d in range(1, GROUP):
            rs_copy(q, d).wait_recv()
        value = own[q, pl.ds(pl.multiple_of(low * share, share), share), :]
        for d in range(1, GROUP):
            value = value + slots[q, d]
        if groups > 1:
            far[q, high] = value
            for e in range(1, groups):
                begin(far_copy(q, e))
            for e in range(1, groups):
                source = lax.rem(high + groups - e, groups)
                remote(
                    far.at[q, source], far.at[q, source],
                    far_send.at[q, e], far_recv.at[q, e], (s, far_tile(e)),
                ).wait_recv()
            value = far[q, 0]
            for e in range(1, groups):
                value = value + far[q, e]
        out_ref[comp, shard(q, low), :] = value / math.sqrt(cell_total)
        for d in range(1, GROUP):
            begin(ag_copy(q, d))

    def back_side(q):
        for d in range(1, GROUP):
            place = out_ref.at[comp, shard(q, lax.rem(low + GROUP - d, GROUP))]
            remote(
                place, place, ag_send.at[q, d], ag_recv.at[q, d], (s, group_tile(d))
            ).wait_recv()
        begin(agx_copy(q))

    def back_core(q):
        place = out_ref.at[2 * core + 1 - side, span(q)]
        remote(place, place, agx_send.at[q], agx_recv.at[q], other_side).wait_recv()
        begin(agc_copy(q))

    def finish(q):
        place = out_ref.at[pl.ds(2 * (1 - core), 2), span(q)]
        remote(place, place, agc_send.at[q], agc_recv.at[q], other_core).wait_recv()

    stages = [project, over_core, over_side, over_tiles, back_side, back_core, finish]
    expected = (0.0, 1.2, 3.5, 6.8, 10.1, 12.4, 13.6)
    for _, q, index in sorted(
        (SPACING * q + expected[index], q, index)
        for q in range(chunks)
        for index in range(len(stages))
    ):
        stages[index](q)
    for copy in sends:
        copy.wait_send()


def on_device(sectors, tiles, snapshots, density, sound_speed, offsets, rotation):
    comps, cells, snaps = snapshots.shape
    gather_rotation = rotation.shape[0] % 16 == 0
    if not gather_rotation:
        rotation = lax.all_gather(rotation, "tile", axis=0, tiled=True)
    modes = rotation.shape[1]
    chunks = snaps // CHUNK
    share = CHUNK // GROUP
    groups = tiles // GROUP
    wide = -(-cells // 128) * 128
    f32, bf16 = jnp.float32, jnp.bfloat16
    dma = pltpu.SemaphoreType.DMA
    vmem = pl.BlockSpec(memory_space=pltpu.VMEM)
    hbm = pl.BlockSpec(memory_space=pltpu.HBM)
    return pl.pallas_call(
        functools.partial(kernel, sectors, tiles, gather_rotation),
        out_shape=jax.ShapeDtypeStruct((comps, snaps, modes), f32),
        in_specs=[hbm] * 5,
        out_specs=vmem,
        scratch_shapes=[
            pltpu.VMEM((1, cells), f32),
            pltpu.VMEM((1, cells), f32),
            pltpu.VMEM((1, cells), jnp.int32),
            pltpu.VMEM((comps, cells + 2 * HALO, snaps), bf16),
            pltpu.VMEM((8, wide), f32),
            pltpu.VMEM((comps, cells, snaps), bf16),
            pltpu.VMEM((comps, cells, modes), bf16),
            pltpu.VMEM((snaps, modes), bf16),
            pltpu.VMEM((comps, snaps, modes), f32),
            pltpu.VMEM((chunks, 2, CHUNK, modes), f32),
            pltpu.VMEM((chunks, CHUNK, modes), f32),
            pltpu.VMEM((chunks, CHUNK, modes), f32),
            pltpu.VMEM((chunks, CHUNK, modes), f32),
            pltpu.VMEM((chunks, GROUP, share, modes), f32),
            pltpu.VMEM((chunks, groups, share, modes), f32),
            dma((comps,)),
            dma((3,)),
            dma((1,)),
            dma((2,)),
            dma((2,)),
            dma((tiles,)),
            dma((tiles,)),
            dma((chunks,)),
            dma((chunks,)),
            dma((chunks,)),
            dma((chunks,)),
            dma((chunks, GROUP)),
            dma((chunks, GROUP)),
            dma((chunks, groups)),
            dma((chunks, groups)),
            dma((chunks, GROUP)),
            dma((chunks, GROUP)),
            dma((chunks,)),
            dma((chunks,)),
            dma((chunks,)),
            dma((chunks,)),
        ],
        compiler_params=pltpu.CompilerParams(
            collective_id=0, has_side_effects=True, vmem_limit_bytes=64 * 1024 * 1024
        ),
        cost_estimate=pl.CostEstimate(
            flops=4 * cells * comps * snaps * modes, bytes_accessed=2 * comps * cells * snaps,
            transcendentals=0,
        ),
    )(snapshots, density[None], sound_speed[None], offsets[None], rotation)


def solution(mesh):
    sectors, tiles = mesh.shape["sector"], mesh.shape["tile"]
    return jax.shard_map(
        functools.partial(on_device, sectors, tiles),
        mesh=mesh,
        in_specs=(
            P(None, ("sector", "tile"), None),
            P(("sector", "tile")),
            P(("sector", "tile")),
            P(("sector", "tile")),
            P("tile", None),
        ),
        out_specs=P(),
        check_vma=False,
    )
```

```python
import functools
import math

import jax
import jax.numpy as jnp
from jax import lax
from jax.experimental import pallas as pl
from jax.experimental.pallas import tpu as pltpu
from jax.sharding import PartitionSpec as P

HALO = 32
GROUP = 8
BLOCK = 192
CHUNK = 128
SPACING = 1.5
MESH = pl.DeviceIdType.MESH


def remote(src, dst, send_sem, recv_sem, device):
    return pltpu.make_async_remote_copy(
        src_ref=src,
        dst_ref=dst,
        send_sem=send_sem,
        recv_sem=recv_sem,
        device_id=device,
        device_id_type=MESH,
    )


def kernel(
    sectors, tiles, gather_rotation,
    snap_ref, dens_ref, speed_ref, off_ref, rot_ref,
    out_ref,
    dens_in, speed_in, off_in, pad, rows, columns, weighted, fields, rot_all, part, core_in, x_out, x_in, own, slots, far,
    load_sem, cell_sem, own_rot_sem, halo_send, halo_recv, rot_send, rot_recv, core_send, core_recv, x_send, x_recv,
    rs_send, rs_recv, far_send, far_recv, ag_send, ag_recv, agx_send, agx_recv, agc_send, agc_recv,
):
    comps, cells, snaps = snap_ref.shape
    chunks = snaps // CHUNK
    share = CHUNK // GROUP
    groups = tiles // GROUP

    s = lax.axis_index("sector")
    t = lax.axis_index("tile")
    core = lax.rem(s, 2)
    side = s // 2
    low = lax.rem(t, GROUP)
    high = t // GROUP
    comp = 2 * core + side
    other_core = (s + 1 - 2 * core, t)
    other_side = (lax.rem(s + 2, sectors), t)

    def group_tile(step):
        return high * GROUP + lax.rem(low + step, GROUP)

    def far_tile(step):
        return lax.rem(high + step, groups) * GROUP + low

    me = s * tiles + t
    total = sectors * tiles
    right_index = lax.rem(me + 1, total)
    left_index = lax.rem(me + total - 1, total)
    right = (right_index // tiles, lax.rem(right_index, tiles))
    left = (left_index // tiles, lax.rem(left_index, tiles))

    loads = [
        pltpu.make_async_copy(
            snap_ref.at[c], pad.at[c, pl.ds(HALO, cells)], load_sem.at[c]
        )
        for c in range(comps)
    ]
    cell_loads = [
        pltpu.make_async_copy(source, target, cell_sem.at[i])
        for i, (source, target) in enumerate(
            ((dens_ref, dens_in), (speed_ref, speed_in), (off_ref, off_in))
        )
    ]
    for load in cell_loads + loads:
        load.start()

    peers = [left, right, other_core, other_side]
    peers += [(s, group_tile(d)) for d in range(1, GROUP)]
    peers += [(s, far_tile(e)) for e in range(1, groups)]
    barrier = pltpu.get_barrier_semaphore()
    for peer in peers:
        pl.semaphore_signal(barrier, inc=1, device_id=peer, device_id_type=MESH)

    rows[...] = jnp.zeros_like(rows)
    for load in cell_loads:
        load.wait()
    dens = dens_in[...]
    speed = speed_in[...]
    rows[0:1, 0:cells] = dens
    rows[1:2, 0:cells] = 1.0 / (dens * speed * speed)
    rows[2:3, 0:cells] = 0.5 / speed
    rows[3:4, 0:cells] = off_in[...].astype(jnp.float32) + HALO
    columns[...] = rows[...].T

    pl.semaphore_wait(barrier, len(peers))
    sends = []
    depth = rot_ref.shape[0]
    if gather_rotation:
        def rot_at(tile):
            return pl.ds(pl.multiple_of(tile * depth, 16), depth)

        for d in range(1, tiles):
            copy = remote(
                rot_ref, rot_all.at[rot_at(t)], rot_send.at[d], rot_recv.at[d],
                (s, lax.rem(t + d, tiles)),
            )
            copy.start()
            sends.append(copy)
        own_rot = pltpu.make_async_copy(rot_ref, rot_all.at[rot_at(t)], own_rot_sem.at[0])
    else:
        own_rot = pltpu.make_async_copy(rot_ref, rot_all, own_rot_sem.at[0])
    own_rot.start()
    to_right = remote(
        snap_ref.at[:, pl.ds(cells - HALO, HALO)], pad.at[:, pl.ds(0, HALO)],
        halo_send.at[0], halo_recv.at[0], right,
    )
    to_left = remote(
        snap_ref.at[:, pl.ds(0, HALO)], pad.at[:, pl.ds(HALO + cells, HALO)],
        halo_send.at[1], halo_recv.at[1], left,
    )
    to_right.start()
    to_left.start()
    sends += [to_right, to_left]

    window = BLOCK + 2 * HALO
    shift = (
        lax.broadcasted_iota(jnp.int32, (BLOCK, window), 1)
        - lax.broadcasted_iota(jnp.int32, (BLOCK, window), 0)
    ).astype(jnp.float32)
    own_cell = jnp.where(shift == HALO, 1.0, 0.0)

    def weigh(block):
        first = pl.multiple_of(block * BLOCK, 16)
        own_rows = pl.ds(first, BLOCK)
        center = pl.ds(pl.multiple_of(first + HALO, 16), BLOCK)
        column = columns[own_rows, :]
        dens_c, inverse, slope, target = (column[:, i : i + 1] for i in range(4))
        pick = (jnp.where(shift == target, 1.0, 0.0) - own_cell).astype(jnp.bfloat16)

        def change(c):
            return jnp.dot(
                pick, pad[c, pl.ds(first, window), :], preferred_element_type=jnp.float32
            )

        def local(c):
            return pad[c, center, :].astype(jnp.float32)

        d_sum = (change(1) + change(2)) + change(3)
        weighted[0, own_rows, :] = (local(0) * inverse + d_sum * slope).astype(jnp.bfloat16)
        push = change(0) * slope
        for c in range(1, comps):
            weighted[c, own_rows, :] = (dens_c * local(c) + push).astype(jnp.bfloat16)

    for load in loads:
        load.wait()
    blocks = cells // BLOCK

    @pl.loop(1, blocks - 1)
    def _(block):
        weigh(block)

    if gather_rotation:
        for d in range(1, tiles):
            source = lax.rem(t + tiles - d, tiles)
            remote(
                rot_ref, rot_all.at[rot_at(source)], rot_send.at[d], rot_recv.at[d],
                (s, source),
            ).wait_recv()
    own_rot.wait()

    @pl.loop(0, comps)
    def _(c):
        fields[c] = jnp.dot(
            pad[c, HALO : HALO + cells, :], rot_all[...], preferred_element_type=jnp.float32
        ).astype(jnp.bfloat16)

    to_right.wait_recv()
    to_left.wait_recv()

    @pl.loop(0, 2)
    def _(end):
        weigh(end * (blocks - 1))

    def span(q):
        return pl.ds(q * CHUNK, CHUNK)

    def shard(q, lo):
        return pl.ds(pl.multiple_of(q * CHUNK + lo * share, share), share)

    def core_copy(q):
        return remote(
            part.at[pl.ds(2 * (1 - core), 2), span(q)], core_in.at[q],
            core_send.at[q], core_recv.at[q], other_core,
        )

    def x_copy(q):
        return remote(x_out.at[q], x_in.at[q], x_send.at[q], x_recv.at[q], other_side)

    def rs_copy(q, d):
        lo = lax.rem(low + d, GROUP)
        return remote(
            own.at[q, pl.ds(pl.multiple_of(lo * share, share), share)], slots.at[q, d],
            rs_send.at[q, d], rs_recv.at[q, d], (s, group_tile(d)),
        )

    def far_copy(q, e):
        return remote(
            far.at[q, high], far.at[q, high],
            far_send.at[q, e], far_recv.at[q, e], (s, far_tile(e)),
        )

    def ag_copy(q, d):
        place = out_ref.at[comp, shard(q, low)]
        return remote(place, place, ag_send.at[q, d], ag_recv.at[q, d], (s, group_tile(d)))

    def agx_copy(q):
        place = out_ref.at[comp, span(q)]
        return remote(place, place, agx_send.at[q], agx_recv.at[q], other_side)

    def agc_copy(q):
        place = out_ref.at[pl.ds(2 * core, 2), span(q)]
        return remote(place, place, agc_send.at[q], agc_recv.at[q], other_core)

    def begin(copy):
        copy.start()
        sends.append(copy)

    def project(q):
        @pl.loop(0, comps)
        def _(c):
            part[c, q * CHUNK : (q + 1) * CHUNK, :] = lax.dot_general(
                weighted[c, :, q * CHUNK : (q + 1) * CHUNK],
                fields[c],
                (((0,), (0,)), ((), ())),
                preferred_element_type=jnp.float32,
            )
        begin(core_copy(q))

    def over_core(q):
        core_copy(q).wait_recv()
        x_out[q] = part[2 * core + 1 - side, q * CHUNK : (q + 1) * CHUNK, :] + core_in[q, 1 - side]
        begin(x_copy(q))
        own[q] = part[comp, q * CHUNK : (q + 1) * CHUNK, :] + core_in[q, side]

    def over_side(q):
        x_copy(q).wait_recv()
        own[q] = own[q] + x_in[q]
        for d in range(1, GROUP):
            begin(rs_copy(q, d))

    def over_tiles(q):
        for d in range(1, GROUP):
            rs_copy(q, d).wait_recv()
        value = own[q, pl.ds(pl.multiple_of(low * share, share), share), :]
        for d in range(1, GROUP):
            value = value + slots[q, d]
        if groups > 1:
            far[q, high] = value
            for e in range(1, groups):
                begin(far_copy(q, e))
            for e in range(1, groups):
                source = lax.rem(high + groups - e, groups)
                remote(
                    far.at[q, source], far.at[q, source],
                    far_send.at[q, e], far_recv.at[q, e], (s, far_tile(e)),
                ).wait_recv()
            value = far[q, 0]
            for e in range(1, groups):
                value = value + far[q, e]
        out_ref[comp, shard(q, low), :] = value
        for d in range(1, GROUP):
            begin(ag_copy(q, d))

    def back_side(q):
        for d in range(1, GROUP):
            place = out_ref.at[comp, shard(q, lax.rem(low + GROUP - d, GROUP))]
            remote(
                place, place, ag_send.at[q, d], ag_recv.at[q, d], (s, group_tile(d))
            ).wait_recv()
        begin(agx_copy(q))

    def back_core(q):
        place = out_ref.at[2 * core + 1 - side, span(q)]
        remote(place, place, agx_send.at[q], agx_recv.at[q], other_side).wait_recv()
        begin(agc_copy(q))

    def finish(q):
        place = out_ref.at[pl.ds(2 * (1 - core), 2), span(q)]
        remote(place, place, agc_send.at[q], agc_recv.at[q], other_core).wait_recv()

    stages = [project, over_core, over_side, over_tiles, back_side, back_core, finish]
    expected = (0.0, 1.2, 3.5, 6.8, 10.1, 12.4, 13.6)
    for _, q, index in sorted(
        (SPACING * q + expected[index], q, index)
        for q in range(chunks)
        for index in range(len(stages))
    ):
        stages[index](q)
    for copy in sends:
        copy.wait_send()


def on_device(sectors, tiles, snapshots, density, sound_speed, offsets, rotation):
    comps, cells, snaps = snapshots.shape
    gather_rotation = rotation.shape[0] % 16 == 0
    if not gather_rotation:
        rotation = lax.all_gather(rotation, "tile", axis=0, tiled=True)
    modes = rotation.shape[1]
    chunks = snaps // CHUNK
    share = CHUNK // GROUP
    groups = tiles // GROUP
    wide = -(-cells // 128) * 128
    f32, bf16 = jnp.float32, jnp.bfloat16
    dma = pltpu.SemaphoreType.DMA
    vmem = pl.BlockSpec(memory_space=pltpu.VMEM)
    hbm = pl.BlockSpec(memory_space=pltpu.HBM)
    summed = pl.pallas_call(
        functools.partial(kernel, sectors, tiles, gather_rotation),
        out_shape=jax.ShapeDtypeStruct((comps, snaps, modes), f32),
        in_specs=[hbm] * 5,
        out_specs=vmem,
        scratch_shapes=[
            pltpu.VMEM((1, cells), f32),
            pltpu.VMEM((1, cells), f32),
            pltpu.VMEM((1, cells), jnp.int32),
            pltpu.VMEM((comps, cells + 2 * HALO, snaps), bf16),
            pltpu.VMEM((8, wide), f32),
            pltpu.VMEM((wide, 8), f32),
            pltpu.VMEM((comps, cells, snaps), bf16),
            pltpu.VMEM((comps, cells, modes), bf16),
            pltpu.VMEM((snaps, modes), bf16),
            pltpu.VMEM((comps, snaps, modes), f32),
            pltpu.VMEM((chunks, 2, CHUNK, modes), f32),
            pltpu.VMEM((chunks, CHUNK, modes), f32),
            pltpu.VMEM((chunks, CHUNK, modes), f32),
            pltpu.VMEM((chunks, CHUNK, modes), f32),
            pltpu.VMEM((chunks, GROUP, share, modes), f32),
            pltpu.VMEM((chunks, groups, share, modes), f32),
            dma((comps,)),
            dma((3,)),
            dma((1,)),
            dma((2,)),
            dma((2,)),
            dma((tiles,)),
            dma((tiles,)),
            dma((chunks,)),
            dma((chunks,)),
            dma((chunks,)),
            dma((chunks,)),
            dma((chunks, GROUP)),
            dma((chunks, GROUP)),
            dma((chunks, groups)),
            dma((chunks, groups)),
            dma((chunks, GROUP)),
            dma((chunks, GROUP)),
            dma((chunks,)),
            dma((chunks,)),
            dma((chunks,)),
            dma((chunks,)),
        ],
        compiler_params=pltpu.CompilerParams(
            collective_id=0, has_side_effects=True, vmem_limit_bytes=64 * 1024 * 1024
        ),
        cost_estimate=pl.CostEstimate(
            flops=4 * cells * comps * snaps * modes, bytes_accessed=2 * comps * cells * snaps,
            transcendentals=0,
        ),
    )(snapshots, density[None], sound_speed[None], offsets[None], rotation)
    return summed / math.sqrt(cells * sectors * tiles)


def solution(mesh):
    sectors, tiles = mesh.shape["sector"], mesh.shape["tile"]
    return jax.shard_map(
        functools.partial(on_device, sectors, tiles),
        mesh=mesh,
        in_specs=(
            P(None, ("sector", "tile"), None),
            P(("sector", "tile")),
            P(("sector", "tile")),
            P(("sector", "tile")),
            P("tile", None),
        ),
        out_specs=P(),
        check_vma=False,
    )
```

```python
import functools
import math

import jax
import jax.numpy as jnp
from jax import lax
from jax.experimental import pallas as pl
from jax.experimental.pallas import tpu as pltpu
from jax.sharding import PartitionSpec as P

HALO = 32
GROUP = 8
DEEP = 4
BLOCK = 192
CHUNK = 128
SPACING = 1.5
MESH = pl.DeviceIdType.MESH


def remote(src, dst, send_sem, recv_sem, device):
    return pltpu.make_async_remote_copy(
        src_ref=src,
        dst_ref=dst,
        send_sem=send_sem,
        recv_sem=recv_sem,
        device_id=device,
        device_id_type=MESH,
    )


def kernel(
    sectors, tiles, gather_rotation,
    snap_ref, dens_ref, speed_ref, off_ref, rot_ref,
    out_ref,
    dens_in, speed_in, off_in, pad, rows, weighted, fields, rot_all, part, core_in, first_out, first_in, own, half_in, slots, far,
    load_sem, cell_sem, own_rot_sem, halo_send, halo_recv, rot_send, rot_recv, core_send, core_recv, first_send, first_recv,
    half_send, half_recv, rs_send, rs_recv, far_send, far_recv, ag_send, ag_recv,
    back_half_send, back_half_recv, back_first_send, back_first_recv, agc_send, agc_recv,
):
    comps, cells, snaps = snap_ref.shape
    chunks = snaps // CHUNK
    share = CHUNK // GROUP
    groups = tiles // GROUP
    cell_total = cells * sectors * tiles

    s = lax.axis_index("sector")
    t = lax.axis_index("tile")
    core = lax.rem(s, 2)
    side = s // 2
    low = lax.rem(t, GROUP)
    high = t // GROUP
    near = lax.rem(low, 2)
    level = low // 2
    other_core = (s + 1 - 2 * core, t)
    other_side = (lax.rem(s + 2, sectors), t)

    other_near = (s, t + 1 - 2 * near)

    def level_tile(step):
        return high * GROUP + 2 * lax.rem(level + step, DEEP) + near

    def far_tile(step):
        return lax.rem(high + step, groups) * GROUP + low

    me = s * tiles + t
    total = sectors * tiles
    right_index = lax.rem(me + 1, total)
    left_index = lax.rem(me + total - 1, total)
    right = (right_index // tiles, lax.rem(right_index, tiles))
    left = (left_index // tiles, lax.rem(left_index, tiles))

    loads = [
        pltpu.make_async_copy(
            snap_ref.at[c], pad.at[c, pl.ds(HALO, cells)], load_sem.at[c]
        )
        for c in range(comps)
    ]
    cell_loads = [
        pltpu.make_async_copy(source, target, cell_sem.at[i])
        for i, (source, target) in enumerate(
            ((dens_ref, dens_in), (speed_ref, speed_in), (off_ref, off_in))
        )
    ]
    for load in cell_loads + loads:
        load.start()

    peers = [left, right, other_core, other_side]
    if gather_rotation:
        peers += [(s, lax.rem(t + d, tiles)) for d in range(1, tiles)]
    else:
        peers += [other_near] + [(s, level_tile(d)) for d in range(1, DEEP)]
    peers += [(s, far_tile(e)) for e in range(1, groups)]
    barrier = pltpu.get_barrier_semaphore()
    for peer in peers:
        pl.semaphore_signal(barrier, inc=1, device_id=peer, device_id_type=MESH)

    rows[...] = jnp.zeros_like(rows)
    for load in cell_loads:
        load.wait()
    dens = dens_in[...]
    speed = speed_in[...]
    rows[0:1, 0:cells] = dens
    rows[1:2, 0:cells] = 1.0 / (dens * speed * speed)
    rows[2:3, 0:cells] = 0.5 / speed
    rows[3:4, 0:cells] = off_in[...].astype(jnp.float32) + HALO
    columns = rows[...].T

    pl.semaphore_wait(barrier, len(peers))
    sends = []
    depth = rot_ref.shape[0]
    if gather_rotation:
        def rot_at(tile):
            return pl.ds(pl.multiple_of(tile * depth, 16), depth)

        for d in range(1, tiles):
            copy = remote(
                rot_ref, rot_all.at[rot_at(t)], rot_send.at[d], rot_recv.at[d],
                (s, lax.rem(t + d, tiles)),
            )
            copy.start()
            sends.append(copy)
        own_rot = pltpu.make_async_copy(rot_ref, rot_all.at[rot_at(t)], own_rot_sem.at[0])
    else:
        own_rot = pltpu.make_async_copy(rot_ref, rot_all, own_rot_sem.at[0])
    own_rot.start()
    to_right = remote(
        snap_ref.at[:, pl.ds(cells - HALO, HALO)], pad.at[:, pl.ds(0, HALO)],
        halo_send.at[0], halo_recv.at[0], right,
    )
    to_left = remote(
        snap_ref.at[:, pl.ds(0, HALO)], pad.at[:, pl.ds(HALO + cells, HALO)],
        halo_send.at[1], halo_recv.at[1], left,
    )
    to_right.start()
    to_left.start()
    sends += [to_right, to_left]

    window = BLOCK + 2 * HALO
    shift = (
        lax.broadcasted_iota(jnp.int32, (BLOCK, window), 1)
        - lax.broadcasted_iota(jnp.int32, (BLOCK, window), 0)
    ).astype(jnp.float32)
    own_cell = jnp.where(shift == HALO, 1.0, 0.0)

    def weigh(block, q):
        first = block * BLOCK
        lanes = slice(q * CHUNK, (q + 1) * CHUNK)
        column = columns[first : first + BLOCK]
        dens_c, inverse, slope, target = (column[:, i : i + 1] for i in range(4))
        pick = (jnp.where(shift == target, 1.0, 0.0) - own_cell).astype(jnp.bfloat16)

        def change(c):
            return jnp.dot(
                pick, pad[c, first : first + window, lanes], preferred_element_type=jnp.float32
            )

        def local(c):
            return pad[c, HALO + first : HALO + first + BLOCK, lanes].astype(jnp.float32)

        d_sum = (change(1) + change(2)) + change(3)
        weighted[0, first : first + BLOCK, lanes] = (
            local(0) * inverse + d_sum * slope
        ).astype(jnp.bfloat16)
        push = change(0) * slope
        for c in range(1, comps):
            weighted[c, first : first + BLOCK, lanes] = (dens_c * local(c) + push).astype(
                jnp.bfloat16
            )

    for load in loads:
        load.wait()
    blocks = cells // BLOCK
    for block in range(1, blocks - 1):
        weigh(block, 0)

    if gather_rotation:
        for d in range(1, tiles):
            source = lax.rem(t + tiles - d, tiles)
            remote(
                rot_ref, rot_all.at[rot_at(source)], rot_send.at[d], rot_recv.at[d],
                (s, source),
            ).wait_recv()
    own_rot.wait()
    for c in range(comps):
        fields[c] = jnp.dot(
            pad[c, HALO : HALO + cells, :], rot_all[...], preferred_element_type=jnp.float32
        ).astype(jnp.bfloat16)

    to_right.wait_recv()
    to_left.wait_recv()
    weigh(0, 0)
    weigh(blocks - 1, 0)

    def span(q):
        return pl.ds(q * CHUNK, CHUNK)

    half = CHUNK // 2

    def bits(q):
        return (side, near) if q % 2 == 0 else (near, side)

    def partners(q):
        return (other_side, other_near) if q % 2 == 0 else (other_near, other_side)

    def kept(q):
        return 2 * core + bits(q)[0]

    def given(q):
        return 2 * core + 1 - bits(q)[0]

    def half_span(bit, base=0):
        return pl.ds(pl.multiple_of(base + bit * half, share), half)

    def shard(q, z, base=0):
        return pl.ds(pl.multiple_of(base + bits(q)[1] * half + z * share, share), share)

    def core_copy(q):
        return remote(
            part.at[pl.ds(2 * (1 - core), 2), span(q)], core_in.at[q],
            core_send.at[q], core_recv.at[q], other_core,
        )

    def first_copy(q):
        return remote(
            first_out.at[q], first_in.at[q], first_send.at[q], first_recv.at[q], partners(q)[0]
        )

    def half_copy(q):
        return remote(
            own.at[q, half_span(1 - bits(q)[1])], half_in.at[q],
            half_send.at[q], half_recv.at[q], partners(q)[1],
        )

    def rs_copy(q, d):
        return remote(
            own.at[q, shard(q, lax.rem(level + d, DEEP))], slots.at[q, d],
            rs_send.at[q, d], rs_recv.at[q, d], (s, level_tile(d)),
        )

    def far_copy(q, e):
        return remote(
            far.at[q, high], far.at[q, high],
            far_send.at[q, e], far_recv.at[q, e], (s, far_tile(e)),
        )

    def ag_copy(q, d, z):
        place = out_ref.at[kept(q), shard(q, z, q * CHUNK)]
        return remote(place, place, ag_send.at[q, d], ag_recv.at[q, d], (s, level_tile(d)))

    def back_half_copy(q, bit):
        place = out_ref.at[kept(q), half_span(bit, q * CHUNK)]
        return remote(
            place, place, back_half_send.at[q], back_half_recv.at[q], partners(q)[1]
        )

    def back_first_copy(q, c):
        place = out_ref.at[c, span(q)]
        return remote(
            place, place, back_first_send.at[q], back_first_recv.at[q], partners(q)[0]
        )

    def agc_copy(q, pair):
        place = out_ref.at[pl.ds(2 * pair, 2), span(q)]
        return remote(place, place, agc_send.at[q], agc_recv.at[q], other_core)

    def begin(copy):
        copy.start()
        sends.append(copy)

    def project(q):
        if q > 0:
            for block in range(blocks):
                weigh(block, q)
        for c in range(comps):
            part[c, q * CHUNK : (q + 1) * CHUNK, :] = lax.dot_general(
                weighted[c, :, q * CHUNK : (q + 1) * CHUNK],
                fields[c],
                (((0,), (0,)), ((), ())),
                preferred_element_type=jnp.float32,
            )
        begin(core_copy(q))

    def over_core(q):
        core_copy(q).wait_recv()
        bit = bits(q)[0]
        first_out[q] = part[given(q), q * CHUNK : (q + 1) * CHUNK, :] + core_in[q, 1 - bit]
        begin(first_copy(q))
        own[q] = part[kept(q), q * CHUNK : (q + 1) * CHUNK, :] + core_in[q, bit]

    def over_first(q):
        first_copy(q).wait_recv()
        own[q] = own[q] + first_in[q]
        begin(half_copy(q))

    def over_half(q):
        half_copy(q).wait_recv()
        mine = half_span(bits(q)[1])
        own[q, mine, :] = own[q, mine, :] + half_in[q]
        for d in range(1, DEEP):
            begin(rs_copy(q, d))

    def over_levels(q):
        for d in range(1, DEEP):
            rs_copy(q, d).wait_recv()
        value = own[q, shard(q, level), :]
        for d in range(1, DEEP):
            value = value + slots[q, d]
        if groups > 1:
            far[q, high] = value
            for e in range(1, groups):
                begin(far_copy(q, e))
            for e in range(1, groups):
                source = lax.rem(high + groups - e, groups)
                remote(
                    far.at[q, source], far.at[q, source],
                    far_send.at[q, e], far_recv.at[q, e], (s, far_tile(e)),
                ).wait_recv()
            value = far[q, 0]
            for e in range(1, groups):
                value = value + far[q, e]
        out_ref[kept(q), shard(q, level, q * CHUNK), :] = value / math.sqrt(cell_total)
        for d in range(1, DEEP):
            begin(ag_copy(q, d, level))

    def back_levels(q):
        for d in range(1, DEEP):
            ag_copy(q, d, lax.rem(level + DEEP - d, DEEP)).wait_recv()
        begin(back_half_copy(q, bits(q)[1]))

    def back_half(q):
        back_half_copy(q, 1 - bits(q)[1]).wait_recv()
        begin(back_first_copy(q, kept(q)))

    def back_first(q):
        back_first_copy(q, given(q)).wait_recv()
        begin(agc_copy(q, core))

    def finish(q):
        agc_copy(q, 1 - core).wait_recv()

    stages = [
        project, over_core, over_first, over_half, over_levels,
        back_levels, back_half, back_first, finish,
    ]
    expected = (0.0, 1.2, 3.2, 4.9, 7.0, 9.1, 10.8, 12.8, 14.0)
    for _, q, index in sorted(
        (SPACING * q + expected[index], q, index)
        for q in range(chunks)
        for index in range(len(stages))
    ):
        stages[index](q)
    for copy in sends:
        copy.wait_send()


def on_device(sectors, tiles, snapshots, density, sound_speed, offsets, rotation):
    comps, cells, snaps = snapshots.shape
    gather_rotation = rotation.shape[0] % 16 == 0
    if not gather_rotation:
        rotation = lax.all_gather(rotation, "tile", axis=0, tiled=True)
    modes = rotation.shape[1]
    chunks = snaps // CHUNK
    share = CHUNK // GROUP
    groups = tiles // GROUP
    wide = -(-cells // 128) * 128
    f32, bf16 = jnp.float32, jnp.bfloat16
    dma = pltpu.SemaphoreType.DMA
    vmem = pl.BlockSpec(memory_space=pltpu.VMEM)
    hbm = pl.BlockSpec(memory_space=pltpu.HBM)
    return pl.pallas_call(
        functools.partial(kernel, sectors, tiles, gather_rotation),
        out_shape=jax.ShapeDtypeStruct((comps, snaps, modes), f32),
        in_specs=[hbm] * 5,
        out_specs=vmem,
        scratch_shapes=[
            pltpu.VMEM((1, cells), f32),
            pltpu.VMEM((1, cells), f32),
            pltpu.VMEM((1, cells), jnp.int32),
            pltpu.VMEM((comps, cells + 2 * HALO, snaps), bf16),
            pltpu.VMEM((8, wide), f32),
            pltpu.VMEM((comps, cells, snaps), bf16),
            pltpu.VMEM((comps, cells, modes), bf16),
            pltpu.VMEM((snaps, modes), bf16),
            pltpu.VMEM((comps, snaps, modes), f32),
            pltpu.VMEM((chunks, 2, CHUNK, modes), f32),
            pltpu.VMEM((chunks, CHUNK, modes), f32),
            pltpu.VMEM((chunks, CHUNK, modes), f32),
            pltpu.VMEM((chunks, CHUNK, modes), f32),
            pltpu.VMEM((chunks, CHUNK // 2, modes), f32),
            pltpu.VMEM((chunks, DEEP, share, modes), f32),
            pltpu.VMEM((chunks, groups, share, modes), f32),
            dma((comps,)),
            dma((3,)),
            dma((1,)),
            dma((2,)),
            dma((2,)),
            dma((tiles,)),
            dma((tiles,)),
            dma((chunks,)),
            dma((chunks,)),
            dma((chunks,)),
            dma((chunks,)),
            dma((chunks,)),
            dma((chunks,)),
            dma((chunks, DEEP)),
            dma((chunks, DEEP)),
            dma((chunks, groups)),
            dma((chunks, groups)),
            dma((chunks, DEEP)),
            dma((chunks, DEEP)),
            dma((chunks,)),
            dma((chunks,)),
            dma((chunks,)),
            dma((chunks,)),
            dma((chunks,)),
            dma((chunks,)),
        ],
        compiler_params=pltpu.CompilerParams(
            collective_id=0, has_side_effects=True, vmem_limit_bytes=64 * 1024 * 1024
        ),
        cost_estimate=pl.CostEstimate(
            flops=4 * cells * comps * snaps * modes, bytes_accessed=2 * comps * cells * snaps,
            transcendentals=0,
        ),
    )(snapshots, density[None], sound_speed[None], offsets[None], rotation)


def solution(mesh):
    sectors, tiles = mesh.shape["sector"], mesh.shape["tile"]
    return jax.shard_map(
        functools.partial(on_device, sectors, tiles),
        mesh=mesh,
        in_specs=(
            P(None, ("sector", "tile"), None),
            P(("sector", "tile")),
            P(("sector", "tile")),
            P(("sector", "tile")),
            P("tile", None),
        ),
        out_specs=P(),
        check_vma=False,
    )
```

```python
import functools
import math

import jax
import jax.numpy as jnp
from jax import lax
from jax.experimental import pallas as pl
from jax.experimental.pallas import tpu as pltpu
from jax.sharding import PartitionSpec as P

HALO = 32
GROUP = 8
BLOCK = 192
CHUNK = 128
SPACING = 1.5
MESH = pl.DeviceIdType.MESH


def remote(src, dst, send_sem, recv_sem, device):
    return pltpu.make_async_remote_copy(
        src_ref=src,
        dst_ref=dst,
        send_sem=send_sem,
        recv_sem=recv_sem,
        device_id=device,
        device_id_type=MESH,
    )


def kernel(
    sectors, tiles, gather_rotation,
    snap_ref, dens_ref, speed_ref, off_ref, rot_ref,
    out_ref,
    dens_in, speed_in, off_in, pad, rows, weighted, fields, rot_all, part, core_in, own, slots, far,
    load_sem, cell_sem, own_rot_sem, halo_send, halo_recv, rot_send, rot_recv, core_send, core_recv,
    rs_send, rs_recv, far_send, far_recv, ag_send, ag_recv, agc_send, agc_recv,
):
    comps, cells, snaps = snap_ref.shape
    chunks = snaps // CHUNK
    share = CHUNK // GROUP
    groups = tiles // GROUP
    cell_total = cells * sectors * tiles

    s = lax.axis_index("sector")
    t = lax.axis_index("tile")
    core = lax.rem(s, 2)
    side = s // 2
    low = lax.rem(t, GROUP)
    high = t // GROUP
    comp = 2 * core + side
    other_core = (s + 1 - 2 * core, t)
    other_side = (lax.rem(s + 2, sectors), t)

    def group_tile(step):
        return high * GROUP + lax.rem(low + step, GROUP)

    def holder(step):
        sector = s if step < GROUP else lax.rem(s + 2, sectors)
        return (sector, group_tile(step % GROUP))

    def far_tile(step):
        return lax.rem(high + step, groups) * GROUP + low

    me = s * tiles + t
    total = sectors * tiles
    right_index = lax.rem(me + 1, total)
    left_index = lax.rem(me + total - 1, total)
    right = (right_index // tiles, lax.rem(right_index, tiles))
    left = (left_index // tiles, lax.rem(left_index, tiles))

    loads = [
        pltpu.make_async_copy(
            snap_ref.at[c], pad.at[c, pl.ds(HALO, cells)], load_sem.at[c]
        )
        for c in range(comps)
    ]
    cell_loads = [
        pltpu.make_async_copy(source, target, cell_sem.at[i])
        for i, (source, target) in enumerate(
            ((dens_ref, dens_in), (speed_ref, speed_in), (off_ref, off_in))
        )
    ]
    for load in cell_loads + loads:
        load.start()

    peers = [left, right, other_core, other_side]
    peers += [(s, group_tile(d)) for d in range(1, GROUP)]
    peers += [holder(GROUP + d) for d in range(1, GROUP)]
    peers += [(s, far_tile(e)) for e in range(1, groups)]
    barrier = pltpu.get_barrier_semaphore()
    for peer in peers:
        pl.semaphore_signal(barrier, inc=1, device_id=peer, device_id_type=MESH)

    rows[...] = jnp.zeros_like(rows)
    for load in cell_loads:
        load.wait()
    dens = dens_in[...]
    speed = speed_in[...]
    rows[0:1, 0:cells] = dens
    rows[1:2, 0:cells] = 1.0 / (dens * speed * speed)
    rows[2:3, 0:cells] = 0.5 / speed
    rows[3:4, 0:cells] = off_in[...].astype(jnp.float32) + HALO
    columns = rows[...].T

    pl.semaphore_wait(barrier, len(peers))
    sends = []
    depth = rot_ref.shape[0]
    if gather_rotation:
        def rot_at(tile):
            return pl.ds(pl.multiple_of(tile * depth, 16), depth)

        for d in range(1, tiles):
            copy = remote(
                rot_ref, rot_all.at[rot_at(t)], rot_send.at[d], rot_recv.at[d],
                (s, lax.rem(t + d, tiles)),
            )
            copy.start()
            sends.append(copy)
        own_rot = pltpu.make_async_copy(rot_ref, rot_all.at[rot_at(t)], own_rot_sem.at[0])
    else:
        own_rot = pltpu.make_async_copy(rot_ref, rot_all, own_rot_sem.at[0])
    own_rot.start()
    to_right = remote(
        snap_ref.at[:, pl.ds(cells - HALO, HALO)], pad.at[:, pl.ds(0, HALO)],
        halo_send.at[0], halo_recv.at[0], right,
    )
    to_left = remote(
        snap_ref.at[:, pl.ds(0, HALO)], pad.at[:, pl.ds(HALO + cells, HALO)],
        halo_send.at[1], halo_recv.at[1], left,
    )
    to_right.start()
    to_left.start()
    sends += [to_right, to_left]

    window = BLOCK + 2 * HALO
    shift = (
        lax.broadcasted_iota(jnp.int32, (BLOCK, window), 1)
        - lax.broadcasted_iota(jnp.int32, (BLOCK, window), 0)
    ).astype(jnp.float32)
    own_cell = jnp.where(shift == HALO, 1.0, 0.0)

    def weigh(block, q):
        first = block * BLOCK
        lanes = slice(q * CHUNK, (q + 1) * CHUNK)
        column = columns[first : first + BLOCK]
        dens_c, inverse, slope, target = (column[:, i : i + 1] for i in range(4))
        pick = (jnp.where(shift == target, 1.0, 0.0) - own_cell).astype(jnp.bfloat16)

        def change(c):
            return jnp.dot(
                pick, pad[c, first : first + window, lanes], preferred_element_type=jnp.float32
            )

        def local(c):
            return pad[c, HALO + first : HALO + first + BLOCK, lanes].astype(jnp.float32)

        d_sum = (change(1) + change(2)) + change(3)
        weighted[0, first : first + BLOCK, lanes] = (
            local(0) * inverse + d_sum * slope
        ).astype(jnp.bfloat16)
        push = change(0) * slope
        for c in range(1, comps):
            weighted[c, first : first + BLOCK, lanes] = (dens_c * local(c) + push).astype(
                jnp.bfloat16
            )

    for load in loads:
        load.wait()
    blocks = cells // BLOCK
    for block in range(1, blocks - 1):
        weigh(block, 0)

    if gather_rotation:
        for d in range(1, tiles):
            source = lax.rem(t + tiles - d, tiles)
            remote(
                rot_ref, rot_all.at[rot_at(source)], rot_send.at[d], rot_recv.at[d],
                (s, source),
            ).wait_recv()
    own_rot.wait()
    for c in range(comps):
        fields[c] = jnp.dot(
            pad[c, HALO : HALO + cells, :], rot_all[...], preferred_element_type=jnp.float32
        ).astype(jnp.bfloat16)

    to_right.wait_recv()
    to_left.wait_recv()
    weigh(0, 0)
    weigh(blocks - 1, 0)

    def span(q):
        return pl.ds(q * CHUNK, CHUNK)

    def shard(q, lo):
        return pl.ds(pl.multiple_of(q * CHUNK + lo * share, share), share)

    def core_copy(q):
        return remote(
            part.at[pl.ds(2 * (1 - core), 2), span(q)], core_in.at[q],
            core_send.at[q], core_recv.at[q], other_core,
        )

    def rs_copy(q, d):
        lo = lax.rem(low + d, GROUP)
        slab = side if d < GROUP else 1 - side
        return remote(
            own.at[q, slab, pl.ds(pl.multiple_of(lo * share, share), share)], slots.at[q, d],
            rs_send.at[q, d], rs_recv.at[q, d], holder(d),
        )

    def far_copy(q, e):
        return remote(
            far.at[q, high], far.at[q, high],
            far_send.at[q, e], far_recv.at[q, e], (s, far_tile(e)),
        )

    def ag_copy(q, d, c, lo):
        place = out_ref.at[c, shard(q, lo)]
        return remote(place, place, ag_send.at[q, d], ag_recv.at[q, d], holder(d))

    def agc_copy(q):
        place = out_ref.at[pl.ds(2 * core, 2), span(q)]
        return remote(place, place, agc_send.at[q], agc_recv.at[q], other_core)

    def begin(copy):
        copy.start()
        sends.append(copy)

    def project(q):
        if q > 0:
            for block in range(blocks):
                weigh(block, q)
        for c in range(comps):
            part[c, q * CHUNK : (q + 1) * CHUNK, :] = lax.dot_general(
                weighted[c, :, q * CHUNK : (q + 1) * CHUNK],
                fields[c],
                (((0,), (0,)), ((), ())),
                preferred_element_type=jnp.float32,
            )
        begin(core_copy(q))

    def over_core(q):
        core_copy(q).wait_recv()
        own[q] = part[pl.ds(2 * core, 2), q * CHUNK : (q + 1) * CHUNK, :] + core_in[q]
        for d in range(1, 2 * GROUP):
            begin(rs_copy(q, d))

    def over_tiles(q):
        for d in range(1, 2 * GROUP):
            rs_copy(q, d).wait_recv()
        value = own[q, side, pl.ds(pl.multiple_of(low * share, share), share), :]
        for d in range(1, 2 * GROUP):
            value = value + slots[q, d]
        if groups > 1:
            far[q, high] = value
            for e in range(1, groups):
                begin(far_copy(q, e))
            for e in range(1, groups):
                source = lax.rem(high + groups - e, groups)
                remote(
                    far.at[q, source], far.at[q, source],
                    far_send.at[q, e], far_recv.at[q, e], (s, far_tile(e)),
                ).wait_recv()
            value = far[q, 0]
            for e in range(1, groups):
                value = value + far[q, e]
        out_ref[comp, shard(q, low), :] = value / math.sqrt(cell_total)
        for d in range(1, 2 * GROUP):
            begin(ag_copy(q, d, comp, low))

    def back_core(q):
        for d in range(1, 2 * GROUP):
            source = comp if d < GROUP else 2 * core + 1 - side
            ag_copy(q, d, source, lax.rem(low + GROUP - d % GROUP, GROUP)).wait_recv()
        begin(agc_copy(q))

    def finish(q):
        place = out_ref.at[pl.ds(2 * (1 - core), 2), span(q)]
        remote(place, place, agc_send.at[q], agc_recv.at[q], other_core).wait_recv()

    stages = [project, over_core, over_tiles, back_core, finish]
    expected = (0.0, 1.3, 6.0, 11.0, 12.3)
    for _, q, index in sorted(
        (SPACING * q + expected[index], q, index)
        for q in range(chunks)
        for index in range(len(stages))
    ):
        stages[index](q)
    for copy in sends:
        copy.wait_send()


def on_device(sectors, tiles, snapshots, density, sound_speed, offsets, rotation):
    comps, cells, snaps = snapshots.shape
    gather_rotation = rotation.shape[0] % 16 == 0
    if not gather_rotation:
        rotation = lax.all_gather(rotation, "tile", axis=0, tiled=True)
    modes = rotation.shape[1]
    chunks = snaps // CHUNK
    share = CHUNK // GROUP
    groups = tiles // GROUP
    wide = -(-cells // 128) * 128
    f32, bf16 = jnp.float32, jnp.bfloat16
    dma = pltpu.SemaphoreType.DMA
    vmem = pl.BlockSpec(memory_space=pltpu.VMEM)
    hbm = pl.BlockSpec(memory_space=pltpu.HBM)
    return pl.pallas_call(
        functools.partial(kernel, sectors, tiles, gather_rotation),
        out_shape=jax.ShapeDtypeStruct((comps, snaps, modes), f32),
        in_specs=[hbm] * 5,
        out_specs=vmem,
        scratch_shapes=[
            pltpu.VMEM((1, cells), f32),
            pltpu.VMEM((1, cells), f32),
            pltpu.VMEM((1, cells), jnp.int32),
            pltpu.VMEM((comps, cells + 2 * HALO, snaps), bf16),
            pltpu.VMEM((8, wide), f32),
            pltpu.VMEM((comps, cells, snaps), bf16),
            pltpu.VMEM((comps, cells, modes), bf16),
            pltpu.VMEM((snaps, modes), bf16),
            pltpu.VMEM((comps, snaps, modes), f32),
            pltpu.VMEM((chunks, 2, CHUNK, modes), f32),
            pltpu.VMEM((chunks, 2, CHUNK, modes), f32),
            pltpu.VMEM((chunks, 2 * GROUP, share, modes), f32),
            pltpu.VMEM((chunks, groups, share, modes), f32),
            dma((comps,)),
            dma((3,)),
            dma((1,)),
            dma((2,)),
            dma((2,)),
            dma((tiles,)),
            dma((tiles,)),
            dma((chunks,)),
            dma((chunks,)),
            dma((chunks, 2 * GROUP)),
            dma((chunks, 2 * GROUP)),
            dma((chunks, groups)),
            dma((chunks, groups)),
            dma((chunks, 2 * GROUP)),
            dma((chunks, 2 * GROUP)),
            dma((chunks,)),
            dma((chunks,)),
        ],
        compiler_params=pltpu.CompilerParams(
            collective_id=0, has_side_effects=True, vmem_limit_bytes=64 * 1024 * 1024
        ),
        cost_estimate=pl.CostEstimate(
            flops=4 * cells * comps * snaps * modes, bytes_accessed=2 * comps * cells * snaps,
            transcendentals=0,
        ),
    )(snapshots, density[None], sound_speed[None], offsets[None], rotation)


def solution(mesh):
    sectors, tiles = mesh.shape["sector"], mesh.shape["tile"]
    return jax.shard_map(
        functools.partial(on_device, sectors, tiles),
        mesh=mesh,
        in_specs=(
            P(None, ("sector", "tile"), None),
            P(("sector", "tile")),
            P(("sector", "tile")),
            P(("sector", "tile")),
            P("tile", None),
        ),
        out_specs=P(),
        check_vma=False,
    )
```

```python
import functools
import math

import jax
import jax.numpy as jnp
from jax import lax
from jax.experimental import pallas as pl
from jax.experimental.pallas import tpu as pltpu
from jax.sharding import PartitionSpec as P

HALO = 32
GROUP = 8
BLOCK = 192
CHUNK = 128
SPACING = 1.5
MESH = pl.DeviceIdType.MESH


def remote(src, dst, send_sem, recv_sem, device):
    return pltpu.make_async_remote_copy(
        src_ref=src,
        dst_ref=dst,
        send_sem=send_sem,
        recv_sem=recv_sem,
        device_id=device,
        device_id_type=MESH,
    )


def kernel(
    sectors, tiles, gather_rotation,
    snap_ref, dens_ref, speed_ref, off_ref, rot_ref,
    out_ref,
    dens_in, speed_in, off_in, pad, rows, weighted, fields, rot_all, part, core_in, own, slots, far,
    load_sem, cell_sem, own_rot_sem, halo_send, halo_recv, rot_send, rot_recv, core_send, core_recv,
    rs_send, rs_recv, far_send, far_recv, ag_send, ag_recv, agc_send, agc_recv,
):
    comps, cells, snaps = snap_ref.shape
    chunks = snaps // CHUNK
    share = CHUNK // GROUP
    groups = tiles // GROUP
    cell_total = cells * sectors * tiles

    s = lax.axis_index("sector")
    t = lax.axis_index("tile")
    core = lax.rem(s, 2)
    side = s // 2
    low = lax.rem(t, GROUP)
    high = t // GROUP
    comp = 2 * core + side
    other_core = (s + 1 - 2 * core, t)
    other_side = (lax.rem(s + 2, sectors), t)

    def group_tile(step):
        return high * GROUP + lax.rem(low + step, GROUP)

    def holder(step):
        sector = s if step < GROUP else lax.rem(s + 2, sectors)
        return (sector, group_tile(step % GROUP))

    def far_tile(step):
        return lax.rem(high + step, groups) * GROUP + low

    me = s * tiles + t
    total = sectors * tiles
    right_index = lax.rem(me + 1, total)
    left_index = lax.rem(me + total - 1, total)
    right = (right_index // tiles, lax.rem(right_index, tiles))
    left = (left_index // tiles, lax.rem(left_index, tiles))

    loads = [
        pltpu.make_async_copy(
            snap_ref.at[c], pad.at[c, pl.ds(HALO, cells)], load_sem.at[c]
        )
        for c in range(comps)
    ]
    cell_loads = [
        pltpu.make_async_copy(source, target, cell_sem.at[i])
        for i, (source, target) in enumerate(
            ((dens_ref, dens_in), (speed_ref, speed_in), (off_ref, off_in))
        )
    ]
    for load in cell_loads + loads:
        load.start()

    peers = [left, right, other_core, other_side]
    peers += [(s, group_tile(d)) for d in range(1, GROUP)]
    peers += [holder(GROUP + d) for d in range(1, GROUP)]
    peers += [(s, far_tile(e)) for e in range(1, groups)]
    barrier = pltpu.get_barrier_semaphore()
    for peer in peers:
        pl.semaphore_signal(barrier, inc=1, device_id=peer, device_id_type=MESH)

    rows[...] = jnp.zeros_like(rows)
    for load in cell_loads:
        load.wait()
    dens = dens_in[...]
    speed = speed_in[...]
    rows[0:1, 0:cells] = dens
    rows[1:2, 0:cells] = 1.0 / (dens * speed * speed)
    rows[2:3, 0:cells] = 0.5 / speed
    rows[3:4, 0:cells] = off_in[...].astype(jnp.float32) + HALO
    columns = rows[...].T

    pl.semaphore_wait(barrier, len(peers))
    sends = []
    depth = rot_ref.shape[0]
    if gather_rotation:
        def rot_at(tile):
            return pl.ds(pl.multiple_of(tile * depth, 16), depth)

        for d in range(1, tiles):
            copy = remote(
                rot_ref, rot_all.at[rot_at(t)], rot_send.at[d], rot_recv.at[d],
                (s, lax.rem(t + d, tiles)),
            )
            copy.start()
            sends.append(copy)
        own_rot = pltpu.make_async_copy(rot_ref, rot_all.at[rot_at(t)], own_rot_sem.at[0])
    else:
        own_rot = pltpu.make_async_copy(rot_ref, rot_all, own_rot_sem.at[0])
    own_rot.start()
    to_right = remote(
        snap_ref.at[:, pl.ds(cells - HALO, HALO)], pad.at[:, pl.ds(0, HALO)],
        halo_send.at[0], halo_recv.at[0], right,
    )
    to_left = remote(
        snap_ref.at[:, pl.ds(0, HALO)], pad.at[:, pl.ds(HALO + cells, HALO)],
        halo_send.at[1], halo_recv.at[1], left,
    )
    to_right.start()
    to_left.start()
    sends += [to_right, to_left]

    window = BLOCK + 2 * HALO
    shift = (
        lax.broadcasted_iota(jnp.int32, (BLOCK, window), 1)
        - lax.broadcasted_iota(jnp.int32, (BLOCK, window), 0)
    ).astype(jnp.float32)
    own_cell = jnp.where(shift == HALO, 1.0, 0.0)

    def weigh(block, q):
        first = block * BLOCK
        lanes = slice(q * CHUNK, (q + 1) * CHUNK)
        column = columns[first : first + BLOCK]
        dens_c, inverse, slope, target = (column[:, i : i + 1] for i in range(4))
        pick = (jnp.where(shift == target, 1.0, 0.0) - own_cell).astype(jnp.bfloat16)

        def change(c):
            return jnp.dot(
                pick, pad[c, first : first + window, lanes], preferred_element_type=jnp.float32
            )

        def local(c):
            return pad[c, HALO + first : HALO + first + BLOCK, lanes].astype(jnp.float32)

        d_sum = (change(1) + change(2)) + change(3)
        weighted[0, first : first + BLOCK, lanes] = (
            local(0) * inverse + d_sum * slope
        ).astype(jnp.bfloat16)
        push = change(0) * slope
        for c in range(1, comps):
            weighted[c, first : first + BLOCK, lanes] = (dens_c * local(c) + push).astype(
                jnp.bfloat16
            )

    for load in loads:
        load.wait()
    blocks = cells // BLOCK
    for q in range(chunks):
        for block in range(1, blocks - 1):
            weigh(block, q)

    if gather_rotation:
        for d in range(1, tiles):
            source = lax.rem(t + tiles - d, tiles)
            remote(
                rot_ref, rot_all.at[rot_at(source)], rot_send.at[d], rot_recv.at[d],
                (s, source),
            ).wait_recv()
    own_rot.wait()
    for c in range(comps):
        fields[c] = jnp.dot(
            pad[c, HALO : HALO + cells, :], rot_all[...], preferred_element_type=jnp.float32
        ).astype(jnp.bfloat16)

    to_right.wait_recv()
    to_left.wait_recv()
    weigh(0, 0)
    weigh(blocks - 1, 0)

    def span(q):
        return pl.ds(q * CHUNK, CHUNK)

    def shard(q, lo):
        return pl.ds(pl.multiple_of(q * CHUNK + lo * share, share), share)

    def core_copy(q):
        return remote(
            part.at[pl.ds(2 * (1 - core), 2), span(q)], core_in.at[q],
            core_send.at[q], core_recv.at[q], other_core,
        )

    def rs_copy(q, d):
        lo = lax.rem(low + d, GROUP)
        slab = side if d < GROUP else 1 - side
        return remote(
            own.at[q, slab, pl.ds(pl.multiple_of(lo * share, share), share)], slots.at[q, d],
            rs_send.at[q, d], rs_recv.at[q, d], holder(d),
        )

    def far_copy(q, e):
        return remote(
            far.at[q, high], far.at[q, high],
            far_send.at[q, e], far_recv.at[q, e], (s, far_tile(e)),
        )

    def ag_copy(q, d, c, lo):
        place = out_ref.at[c, shard(q, lo)]
        return remote(place, place, ag_send.at[q, d], ag_recv.at[q, d], holder(d))

    def agc_copy(q):
        place = out_ref.at[pl.ds(2 * core, 2), span(q)]
        return remote(place, place, agc_send.at[q], agc_recv.at[q], other_core)

    def begin(copy):
        copy.start()
        sends.append(copy)

    def project(q):
        if q > 0:
            weigh(0, q)
            weigh(blocks - 1, q)
        for c in range(comps):
            part[c, q * CHUNK : (q + 1) * CHUNK, :] = lax.dot_general(
                weighted[c, :, q * CHUNK : (q + 1) * CHUNK],
                fields[c],
                (((0,), (0,)), ((), ())),
                preferred_element_type=jnp.float32,
            )
        begin(core_copy(q))

    def over_core(q):
        core_copy(q).wait_recv()
        own[q] = part[pl.ds(2 * core, 2), q * CHUNK : (q + 1) * CHUNK, :] + core_in[q]
        for d in range(1, 2 * GROUP):
            begin(rs_copy(q, d))

    def over_tiles(q):
        for d in range(1, 2 * GROUP):
            rs_copy(q, d).wait_recv()
        value = own[q, side, pl.ds(pl.multiple_of(low * share, share), share), :]
        for d in range(1, 2 * GROUP):
            value = value + slots[q, d]
        if groups > 1:
            far[q, high] = value
            for e in range(1, groups):
                begin(far_copy(q, e))
            for e in range(1, groups):
                source = lax.rem(high + groups - e, groups)
                remote(
                    far.at[q, source], far.at[q, source],
                    far_send.at[q, e], far_recv.at[q, e], (s, far_tile(e)),
                ).wait_recv()
            value = far[q, 0]
            for e in range(1, groups):
                value = value + far[q, e]
        out_ref[comp, shard(q, low), :] = value / math.sqrt(cell_total)
        for d in range(1, 2 * GROUP):
            begin(ag_copy(q, d, comp, low))

    def back_core(q):
        for d in range(1, 2 * GROUP):
            source = comp if d < GROUP else 2 * core + 1 - side
            ag_copy(q, d, source, lax.rem(low + GROUP - d % GROUP, GROUP)).wait_recv()
        begin(agc_copy(q))

    def finish(q):
        place = out_ref.at[pl.ds(2 * (1 - core), 2), span(q)]
        remote(place, place, agc_send.at[q], agc_recv.at[q], other_core).wait_recv()

    stages = [project, over_core, over_tiles, back_core, finish]
    expected = (0.0, 1.3, 6.0, 11.0, 12.3)
    for _, q, index in sorted(
        (SPACING * q + expected[index], q, index)
        for q in range(chunks)
        for index in range(len(stages))
    ):
        stages[index](q)
    for copy in sends:
        copy.wait_send()


def on_device(sectors, tiles, snapshots, density, sound_speed, offsets, rotation):
    comps, cells, snaps = snapshots.shape
    gather_rotation = rotation.shape[0] % 16 == 0
    if not gather_rotation:
        rotation = lax.all_gather(rotation, "tile", axis=0, tiled=True)
    modes = rotation.shape[1]
    chunks = snaps // CHUNK
    share = CHUNK // GROUP
    groups = tiles // GROUP
    wide = -(-cells // 128) * 128
    f32, bf16 = jnp.float32, jnp.bfloat16
    dma = pltpu.SemaphoreType.DMA
    vmem = pl.BlockSpec(memory_space=pltpu.VMEM)
    hbm = pl.BlockSpec(memory_space=pltpu.HBM)
    return pl.pallas_call(
        functools.partial(kernel, sectors, tiles, gather_rotation),
        out_shape=jax.ShapeDtypeStruct((comps, snaps, modes), f32),
        in_specs=[hbm] * 5,
        out_specs=vmem,
        scratch_shapes=[
            pltpu.VMEM((1, cells), f32),
            pltpu.VMEM((1, cells), f32),
            pltpu.VMEM((1, cells), jnp.int32),
            pltpu.VMEM((comps, cells + 2 * HALO, snaps), bf16),
            pltpu.VMEM((8, wide), f32),
            pltpu.VMEM((comps, cells, snaps), bf16),
            pltpu.VMEM((comps, cells, modes), bf16),
            pltpu.VMEM((snaps, modes), bf16),
            pltpu.VMEM((comps, snaps, modes), f32),
            pltpu.VMEM((chunks, 2, CHUNK, modes), f32),
            pltpu.VMEM((chunks, 2, CHUNK, modes), f32),
            pltpu.VMEM((chunks, 2 * GROUP, share, modes), f32),
            pltpu.VMEM((chunks, groups, share, modes), f32),
            dma((comps,)),
            dma((3,)),
            dma((1,)),
            dma((2,)),
            dma((2,)),
            dma((tiles,)),
            dma((tiles,)),
            dma((chunks,)),
            dma((chunks,)),
            dma((chunks, 2 * GROUP)),
            dma((chunks, 2 * GROUP)),
            dma((chunks, groups)),
            dma((chunks, groups)),
            dma((chunks, 2 * GROUP)),
            dma((chunks, 2 * GROUP)),
            dma((chunks,)),
            dma((chunks,)),
        ],
        compiler_params=pltpu.CompilerParams(
            collective_id=0, has_side_effects=True, vmem_limit_bytes=64 * 1024 * 1024
        ),
        cost_estimate=pl.CostEstimate(
            flops=4 * cells * comps * snaps * modes, bytes_accessed=2 * comps * cells * snaps,
            transcendentals=0,
        ),
    )(snapshots, density[None], sound_speed[None], offsets[None], rotation)


def solution(mesh):
    sectors, tiles = mesh.shape["sector"], mesh.shape["tile"]
    return jax.shard_map(
        functools.partial(on_device, sectors, tiles),
        mesh=mesh,
        in_specs=(
            P(None, ("sector", "tile"), None),
            P(("sector", "tile")),
            P(("sector", "tile")),
            P(("sector", "tile")),
            P("tile", None),
        ),
        out_specs=P(),
        check_vma=False,
    )
```
